512 devices in a mesh: grp: 16 (over z, core), seq: 32 (over y, x).
Axes of the slice: x: 4, y: 8, z: 8, core: 2. Of those that a mesh axis runs over, the one named last changes fastest.
Arguments:
- queries: bfloat16 [32, 32, 64, 1536], P('grp', 'seq'), may hold values from -100 to 100
- keys: bfloat16 [32, 32, 64, 1536], P('grp', 'seq'), may hold values from -5 to 5
- values: bfloat16 [32, 32, 64, 1536], P('grp', 'seq'), may hold values from -6 to 6
- grad_out: bfloat16 [32, 32, 64, 1536], P('grp', 'seq'), may hold values from -6 to 6
- frames: int32 [32], replicated, may hold values from 1 to 32
- timesteps: int32 [32], replicated, may hold values from 0 to 999
- order: int32 [16, 2], replicated, may hold values from 0 to 1, each once within a row
- gate_weight: bfloat16 [256, 1536], replicated, may hold values from -0.375 to 0.375
Outputs:
- attn_out: bfloat16 [32, 32, 64, 1536], P('grp', 'seq')
- grad_q: bfloat16 [32, 32, 64, 1536], P('grp', 'seq')
- grad_k: bfloat16 [32, 32, 64, 1536], P('grp', 'seq')
- grad_v: bfloat16 [32, 32, 64, 1536], P('grp', 'seq')
- grad_gate: bfloat16 [256, 1536], replicated
The draws below stay inside these ranges and needn't reach their ends.
All inputs are finite; a program needn't handle non-finite values.
Results may differ from the reference program's by a relative error of at most 0.012.
Values may be sent and summed in bfloat16 or wider, within the bound.
A program may use at most 64 MiB of HBM per device.

```python
import math
import jax
import jax.numpy as jnp
from jax import lax

HEADS = 12
HD = 128
FREQ = 256
CLIPS_GRP = 2
SPOTS = 64
WIDTH = 1536
CLIPS = 32
FRAMES = 32
N_GRP = 16


def shared_keys(key):
    base = jax.random.normal(jax.random.fold_in(key, 11), (CLIPS, FRAMES, SPOTS, WIDTH), jnp.float32)
    return jnp.clip(base, -5.0, 5.0)


def draw_keys(key, part):
    common = shared_keys(key)
    return common.astype(jnp.bfloat16)


def draw_queries(key, part):
    key = jax.random.fold_in(key, 3)
    first = jax.random.fold_in(key, 0)
    base = jnp.clip(jax.random.normal(first, (CLIPS, FRAMES, SPOTS, WIDTH), jnp.float32), -5.0, 5.0)
    return base.astype(jnp.bfloat16)


def plant(result, rng, smallest, high):
    longest = result.shape.index(max(result.shape))
    spots = []
    for shift in (0, 1):
        where = [jax.random.randint(jax.random.fold_in(rng, axis), (), 0, length) for axis, length in enumerate(result.shape)]
        where[longest] = (where[longest] + shift) % result.shape[longest]
        spots.append(tuple(where))
    return result.at[spots[0]].set(smallest).at[spots[1]].set(high)


def steps_of(rng, shape, cuts, smallest, top_value):
    factor_of = 1.0
    for dim, blocks in cuts:
        heights = jax.random.uniform(jax.random.fold_in(jax.random.fold_in(rng, 6), dim), (blocks,), jnp.float32, smallest / len(cuts), top_value / len(cuts))
        factor_of = factor_of * jnp.repeat(jnp.exp(heights), shape[dim] // blocks).reshape((-1,) + (1,) * (len(shape) - 1 - dim))
    return factor_of


def bell_draw(own_key, dims, scale, limit, shards=(), held_as=jnp.bfloat16):
    drawn = scale * jax.random.normal(own_key, dims, jnp.float32)
    if shards:
        drawn = drawn * steps_of(own_key, dims, shards, -0.22, 0.18)
    return jnp.clip(drawn, -limit, limit).astype(held_as)


def setup_inputs(seed: int = 0) -> dict:
    key_list = jax.random.split(jax.random.key(seed), 9)
    return {
        "queries": draw_queries(jax.random.fold_in(key_list[8], 71), 0),
        "keys": draw_keys(jax.random.fold_in(key_list[8], 71), 0),
        "values": bell_draw(key_list[2], (CLIPS, FRAMES, SPOTS, WIDTH), 1.0, 6.0, ((0, 16), (1, 32))),
        "grad_out": bell_draw(key_list[3], (CLIPS, FRAMES, SPOTS, WIDTH), 1.0, 6.0, ((0, 16), (1, 32))),
        "frames": plant(jax.random.randint(key_list[4], (CLIPS,), 1, FRAMES + 1), jax.random.fold_in(key_list[4], 1), 1, FRAMES).astype(jnp.int32),
        "timesteps": plant(jax.random.randint(key_list[5], (CLIPS,), 0, 1000), jax.random.fold_in(key_list[5], 1), 0, 999).astype(jnp.int32),
        "order": jax.vmap(lambda own: jax.random.permutation(own, CLIPS_GRP))(jax.random.split(key_list[6], N_GRP)).reshape((N_GRP, CLIPS_GRP)).astype(jnp.int32),
        "gate_weight": bell_draw(key_list[7], (FREQ, WIDTH), FREQ ** -0.5, 0.375),
    }


def embed(steps, freq):
    half = freq // 2
    rates = jnp.exp(-math.log(10000.0) * jnp.arange(half, dtype=jnp.float32) / half)
    angle = steps.astype(jnp.float32)[:, None] * rates[None, :]
    return jnp.concatenate([jnp.cos(angle), jnp.sin(angle)], axis=1)


def one_clip(inputs):
    query, key_in, value, cotan, gate_row, count = inputs
    frames_n = query.shape[0]
    spots = query.shape[1]
    scale = HD ** -0.5
    query_h = query.astype(jnp.float32).reshape(frames_n, spots, HEADS, HD)
    key_h = key_in.astype(jnp.float32).reshape(frames_n, spots, HEADS, HD)
    value_h = value.astype(jnp.float32).reshape(frames_n, spots, HEADS, HD)
    position = jnp.arange(frames_n, dtype=jnp.int32)
    live = position < count
    scores = jnp.einsum('ishd,jshd->shij', query_h, key_h) * scale
    masked = jnp.where(live[None, None, None, :], scores, -jnp.inf)
    top = jnp.max(masked, axis=-1, keepdims=True)
    expo = jnp.where(live[None, None, None, :], jnp.exp(masked - top), 0.0)
    probs = expo / jnp.sum(expo, axis=-1, keepdims=True)
    probs_b = probs.astype(jnp.bfloat16).astype(jnp.float32)
    qlive = live.astype(jnp.float32)[:, None, None]
    attn = jnp.einsum('shij,jshd->ishd', probs_b, value_h).reshape(frames_n, spots, -1) * qlive
    attn_out = (gate_row[None, None, :] * attn).astype(jnp.bfloat16)
    cot = cotan.astype(jnp.float32)
    grad_a = (cot * gate_row[None, None, :] * qlive).astype(jnp.bfloat16).astype(jnp.float32)
    grad_a = grad_a.reshape(frames_n, spots, HEADS, HD)
    clip_gate = jnp.sum(cot * attn, axis=(0, 1))
    grad_v = jnp.einsum('shij,ishd->jshd', probs_b, grad_a)
    dprobs = jnp.einsum('ishd,jshd->shij', grad_a, value_h)
    diag = jnp.sum(probs * dprobs, axis=-1, keepdims=True)
    dscores = (probs * (dprobs - diag)).astype(jnp.bfloat16).astype(jnp.float32)
    grad_q = jnp.einsum('shij,jshd->ishd', dscores, key_h) * scale
    grad_k = jnp.einsum('shij,ishd->jshd', dscores, query_h) * scale
    shape = (frames_n, spots, -1)
    return (attn_out, grad_q.reshape(shape).astype(jnp.bfloat16), grad_k.reshape(shape).astype(jnp.bfloat16),
            grad_v.reshape(shape).astype(jnp.bfloat16), clip_gate)


def reference(queries, keys, values, grad_out, frames, timesteps, order, gate_weight):
    half_slots = CLIPS_GRP // 2
    group_ids = jnp.arange(N_GRP, dtype=jnp.int32)[:, None]
    slot_ids = jnp.arange(CLIPS_GRP, dtype=jnp.int32)[None, :]
    partner = jnp.bitwise_xor(group_ids, N_GRP // 2)
    source = jnp.where(slot_ids < half_slots, group_ids, partner)
    source, slot_ids = jnp.broadcast_arrays(source, slot_ids)
    anchor = (source * CLIPS_GRP + order[source, slot_ids]).reshape(-1).astype(jnp.int32)
    embedding = embed(timesteps[anchor], FREQ)
    gate = jnp.dot(embedding, gate_weight.astype(jnp.float32), precision=lax.Precision.HIGHEST)
    results = lax.map(one_clip, (queries[anchor], keys[anchor], values[anchor], grad_out, gate, frames[anchor]))
    grad_gate = jnp.dot(embedding.T, results[4], precision=lax.Precision.HIGHEST).astype(jnp.bfloat16)
    return results[0], results[1], results[2], results[3], grad_gate
```

```python
import functools
import math

import jax
import jax.numpy as jnp
from jax import lax
from jax.experimental import pallas as pl
from jax.experimental.pallas import tpu as pltpu
from jax.sharding import PartitionSpec as P

MESH = pl.DeviceIdType.MESH
HD = 128
ROWS = 16
CUT = 3
GROUPS, RANKS = 16, 32
SPAN = CUT * HD
PACK = 4
SIDE = PACK * RANKS
NT = (((1,), (1,)), ((), ()))
TN = (((0,), (0,)), ((), ()))
NN = (((1,), (0,)), ((), ()))


def dot(a, b, dims):
    return lax.dot_general(a, b, dims, preferred_element_type=jnp.float32)


def exchange(
    frames, steps, order, q_ref, k_ref, v_ref, go_ref, gw_ref,
    outs_ref, sums_ref, emb_ref,
    raw, stage, rin, ob, xf, of, gwv, gate, part, seen, own, everyone,
    load_sem, ssem, rsem, osend, orecv, asend, arecv, bsend, brecv,
):
    g = lax.axis_index("grp")
    me = lax.axis_index("seq")
    partner = lax.rem(g + GROUPS // 2, GROUPS)
    clip = me // 16
    block = lax.rem(me // 4, 4)
    heads = lax.rem(me, 4)

    barrier = pltpu.get_barrier_semaphore()

    def greet(grp, seq):
        pl.semaphore_signal(barrier, inc=1, device_id=(grp, seq), device_id_type=MESH)

    @pl.loop(1, RANKS)
    def _(o):
        greet(g, lax.rem(me + o, RANKS))

    @pl.when(clip == 1)
    def _():
        @pl.loop(0, RANKS)
        def _(o):
            greet(partner, lax.rem(me + o, RANKS))

    @pl.loop(1, GROUPS)
    def _(o):
        greet(lax.rem(g + o, GROUPS), me)

    loads = [
        pltpu.make_async_copy(ref, raw.at[t], load_sem.at[t])
        for t, ref in enumerate((q_ref, k_ref, v_ref))
    ]
    for r in range(2):
        loads.append(pltpu.make_async_copy(go_ref.at[r], stage.at[r, 3], load_sem.at[3 + r]))
    mine = pl.ds(pl.multiple_of(heads * SPAN, HD), SPAN)
    weight = pltpu.make_async_copy(gw_ref.at[:, mine], gwv, load_sem.at[5])
    for load in loads:
        load.start()
    weight.start()
    for load in loads:
        load.wait()
    for t in range(3):
        for r in range(2):
            stage[r, t] = raw[t, order[g, r]]
    pl.semaphore_wait(barrier, RANKS - 1 + 16 + GROUPS - 1)

    def out_to(h, j, t0, n):
        r, b, w = j // 16, lax.rem(j // 4, 4), lax.rem(j, 4)
        return stage.at[
            r,
            pl.ds(t0, n),
            pl.ds(pl.multiple_of(b * ROWS, ROWS), ROWS),
            pl.ds(pl.multiple_of(w * SPAN + h * HD, HD), HD),
        ]

    def slot(h, f, t0, n):
        return rin.at[pl.ds(h * (RANKS * 4) + f * 4 + t0, n)]

    def send(h, j, grp, t0, n):
        pltpu.make_async_remote_copy(
            src_ref=out_to(h, j, t0, n),
            dst_ref=slot(h, me, t0, n),
            send_sem=ssem,
            recv_sem=rsem.at[h],
            device_id=(grp, j),
            device_id_type=MESH,
        ).start()

    def keep(h, t0, n):
        pltpu.make_async_copy(out_to(h, me, t0, n), slot(h, me, t0, n), rsem.at[h]).start()

    @pl.loop(0, CUT)
    def _(h):
        @pl.loop(1, RANKS)
        def _(o):
            j = lax.rem(me + o, RANKS)

            @pl.when(j < 16)
            def _():
                send(h, j, g, 0, 4)

            @pl.when(j >= 16)
            def _():
                send(h, j, partner, 0, 3)
                send(h, j, g, 3, 1)

        @pl.when(clip == 0)
        def _():
            keep(h, 0, 4)

        @pl.when(clip == 1)
        def _():
            send(h, me, partner, 0, 3)
            keep(h, 3, 1)

    half = HD
    row = lax.broadcasted_iota(jnp.int32, (2 * GROUPS, half), 0)
    stamp = jnp.zeros((2 * GROUPS, half), jnp.float32)
    for c in range(2 * GROUPS):
        src = c // 2 if c % 2 == 0 else (c // 2 + GROUPS // 2) % GROUPS
        anchor = src * 2 + order[src, c % 2]
        stamp = jnp.where(row == c, steps[anchor].astype(jnp.float32), stamp)
    k = lax.broadcasted_iota(jnp.int32, (2 * GROUPS, half), 1).astype(jnp.float32)
    angle = stamp * jnp.exp(-math.log(10000.0) * k / half)
    emb_ref[:, :half] = jnp.cos(angle)
    emb_ref[:, half:] = jnp.sin(angle)
    weight.wait()
    gates = lax.dot_general(
        emb_ref[...],
        gwv[...].astype(jnp.float32),
        NN,
        precision=lax.Precision.HIGHEST,
        preferred_element_type=jnp.float32,
    )
    pick = lax.broadcasted_iota(jnp.int32, gates.shape, 0) == g * 2 + clip
    gate[...] = jnp.broadcast_to(
        jnp.sum(jnp.where(pick, gates, 0.0), axis=0, keepdims=True), gate.shape
    )
    source = jnp.where(clip == 0, g, partner)
    count = frames[source * 2 + order[source, clip]]

    line = lax.broadcasted_iota(jnp.int32, (SIDE, SIDE), 0)
    lane = lax.broadcasted_iota(jnp.int32, (SIDE, SIDE), 1)
    live = (line // RANKS == lane // RANKS) & (lax.rem(lane, RANKS) < count)
    asks = (
        lax.rem(lax.broadcasted_iota(jnp.int32, (SIDE, HD), 0), RANKS) < count
    ).astype(jnp.float32)
    scale = HD ** (-0.5)

    @pl.loop(0, CUT)
    def _(h):
        base = h * (RANKS * 4)
        pltpu.make_async_copy(
            rin.at[pl.ds(base, RANKS * 4)], rin.at[pl.ds(base, RANKS * 4)], rsem.at[h]
        ).wait()
        for f in range(RANKS):
            for t in range(4):
                xf[t, f * ROWS : (f + 1) * ROWS, :] = rin[base + f * 4 + t].astype(jnp.float32)
        lanes = pl.ds(pl.multiple_of(h * HD, HD), HD)
        gate_h = gate[0:1, lanes]
        total = jnp.zeros((1, HD), jnp.float32)
        for s in range(ROWS // PACK):

            def take(t):
                return jnp.concatenate(
                    [xf[t, pl.ds(s * PACK + p, RANKS, stride=ROWS), :] for p in range(PACK)], axis=0
                )

            def put(t, value):
                for p in range(PACK):
                    of[t, pl.ds(s * PACK + p, RANKS, stride=ROWS), :] = value[
                        p * RANKS : (p + 1) * RANKS
                    ]

            query = take(0).astype(jnp.bfloat16)
            key = take(1).astype(jnp.bfloat16)
            value = take(2).astype(jnp.bfloat16)
            cotan = take(3)
            scores = jnp.where(live, dot(query, key, NT) * scale, -jnp.inf)
            top = jnp.max(scores, axis=-1, keepdims=True)
            expo = jnp.where(live, jnp.exp(scores - top), 0.0)
            probs = expo / jnp.sum(expo, axis=-1, keepdims=True)
            probs_b = probs.astype(jnp.bfloat16)
            attn = dot(probs_b, value, NN) * asks
            put(0, gate_h * attn)
            total = total + jnp.sum(cotan * attn, axis=0, keepdims=True)
            grad_a = (cotan * gate_h * asks).astype(jnp.bfloat16)
            put(3, dot(probs_b, grad_a, TN))
            dprobs = dot(grad_a, value, NT)
            diag = jnp.sum(probs * dprobs, axis=-1, keepdims=True)
            dscores = (probs * (dprobs - diag)).astype(jnp.bfloat16)
            put(1, dot(dscores, key, NN) * scale)
            put(2, dot(dscores, query, TN) * scale)
        part[0:1, lanes] = total
        for f in range(RANKS):
            for t in range(4):
                ob[base + f * 4 + t] = of[t, f * ROWS : (f + 1) * ROWS, :].astype(jnp.bfloat16)

        @pl.when(h == CUT - 1)
        def _():
            seen[me] = part[...]

            @pl.loop(1, RANKS)
            def _(o):
                pltpu.make_async_remote_copy(
                    src_ref=part,
                    dst_ref=seen.at[me],
                    send_sem=asend,
                    recv_sem=arecv,
                    device_id=(g, lax.rem(me + o, RANKS)),
                    device_id_type=MESH,
                ).start()

        place = outs_ref.at[
            :,
            clip,
            pl.ds(pl.multiple_of(block * ROWS, ROWS), ROWS),
            pl.ds(pl.multiple_of(heads * SPAN + h * HD, HD), HD),
        ]

        @pl.loop(1, RANKS)
        def _(o):
            f = lax.rem(me + o, RANKS)
            pltpu.make_async_remote_copy(
                src_ref=ob.at[pl.ds(base + f * 4, 4)],
                dst_ref=place,
                send_sem=osend,
                recv_sem=orecv,
                device_id=(g, f),
                device_id_type=MESH,
            ).start()

        pltpu.make_async_copy(ob.at[pl.ds(base + me * 4, 4)], place, orecv).start()

    few = seen.at[pl.ds(0, RANKS - 1)]
    pltpu.make_async_copy(few, few, arecv).wait()
    for r in range(2):
        for w in range(4):
            acc = seen[r * 16 + w]
            for b in range(1, 4):
                acc = acc + seen[r * 16 + b * 4 + w]
            own[w * 2 + r : w * 2 + r + 1, :] = acc
    everyone[g] = own[...]

    @pl.loop(1, GROUPS)
    def _(o):
        pltpu.make_async_remote_copy(
            src_ref=own,
            dst_ref=everyone.at[g],
            send_sem=bsend,
            recv_sem=brecv,
            device_id=(lax.rem(g + o, GROUPS), me),
            device_id_type=MESH,
        ).start()

    others = everyone.at[pl.ds(0, GROUPS - 1)]
    pltpu.make_async_copy(others, others, brecv).wait()
    for i in range(GROUPS):
        for w in range(4):
            sums_ref[w, 2 * i : 2 * i + 2, :] = everyone[i, 2 * w : 2 * w + 2, :]

    def drain(sem, ref):
        pltpu.make_async_copy(ref, ref, sem).wait()

    drain(asend, few)
    drain(bsend, others)

    @pl.when(clip == 0)
    def _():
        drain(ssem, rin.at[pl.ds(0, CUT * (15 * 4 + 16 * 4))])

    @pl.when(clip == 1)
    def _():
        drain(ssem, rin.at[pl.ds(0, CUT * (16 * 4 + 15 + 16 * 3))])

    drain(osend, rin.at[pl.ds(0, CUT * (RANKS - 1) * 4)])
    drain(orecv, outs_ref)


def finish(outs_ref, sums_ref, emb_ref, o_ref, q_ref, k_ref, v_ref, gg_ref, sem):
    copies = [
        pltpu.make_async_copy(outs_ref.at[t], ref, sem.at[t])
        for t, ref in enumerate((o_ref, q_ref, k_ref, v_ref))
    ]
    for copy in copies:
        copy.start()
    emb = emb_ref[...]
    for w in range(4):
        clips = sums_ref[w]
        gg_ref[:, w * SPAN : (w + 1) * SPAN] = lax.dot_general(
            emb,
            clips,
            TN,
            precision=lax.Precision.HIGHEST,
            preferred_element_type=jnp.float32,
        ).astype(jnp.bfloat16)
    for copy in copies:
        copy.wait()


def body(queries, keys, values, grad_out, frames, timesteps, order, gate_weight):
    clips, fr_dev, spots, width = queries.shape
    flat = (clips, spots, width)
    any_space = pl.BlockSpec(memory_space=pl.ANY)
    smem = pl.BlockSpec(memory_space=pltpu.SMEM)
    vmem = pl.BlockSpec(memory_space=pltpu.VMEM)
    bf16, f32 = jnp.bfloat16, jnp.float32
    dma = pltpu.SemaphoreType.DMA
    outs, sums, emb = pl.pallas_call(
        exchange,
        out_shape=(
            jax.ShapeDtypeStruct((4,) + flat, bf16),
            jax.ShapeDtypeStruct((4, 2 * GROUPS, SPAN), f32),
            jax.ShapeDtypeStruct((2 * GROUPS, 2 * HD), f32),
        ),
        in_specs=[smem] * 3 + [any_space] * 5,
        out_specs=(any_space, vmem, vmem),
        scratch_shapes=[
            pltpu.VMEM((3,) + flat, bf16),
            pltpu.VMEM((2, 4, spots, width), bf16),
            pltpu.VMEM((CUT * RANKS * 4, ROWS, HD), bf16),
            pltpu.VMEM((CUT * RANKS * 4, ROWS, HD), bf16),
            pltpu.VMEM((4, RANKS * ROWS, HD), f32),
            pltpu.VMEM((4, RANKS * ROWS, HD), f32),
            pltpu.VMEM((gate_weight.shape[0], SPAN), bf16),
            pltpu.VMEM((8, SPAN), f32),
            pltpu.VMEM((1, SPAN), f32),
            pltpu.VMEM((RANKS, 1, SPAN), f32),
            pltpu.VMEM((8, SPAN), f32),
            pltpu.VMEM((GROUPS, 8, SPAN), f32),
            dma((6,)),
            dma,
            dma((CUT,)),
            dma,
            dma,
            dma,
            dma,
            dma,
            dma,
        ],
        compiler_params=pltpu.CompilerParams(
            collective_id=0, has_side_effects=True, vmem_limit_bytes=32 << 20
        ),
    )(
        frames,
        timesteps,
        order,
        queries.reshape(flat),
        keys.reshape(flat),
        values.reshape(flat),
        grad_out.reshape(flat),
        gate_weight,
    )
    results = pl.pallas_call(
        finish,
        out_shape=tuple(jax.ShapeDtypeStruct(flat, bf16) for _ in range(4))
        + (jax.ShapeDtypeStruct(gate_weight.shape, bf16),),
        in_specs=[any_space, vmem, vmem],
        out_specs=(any_space,) * 4 + (vmem,),
        scratch_shapes=[dma((4,))],
        compiler_params=pltpu.CompilerParams(vmem_limit_bytes=32 << 20),
    )(outs, sums, emb)
    back = tuple(x.reshape(clips, fr_dev, spots, width) for x in results[:4])
    return back + (results[4],)


def solution(mesh):
    split = P("grp", "seq", None, None)
    return jax.shard_map(
        body,
        mesh=mesh,
        in_specs=(split,) * 4 + (P(),) * 4,
        out_specs=(split,) * 4 + (P(),),
        check_vma=False,
    )
```

```python
import functools
import math

import jax
import jax.numpy as jnp
from jax import lax
from jax.experimental import pallas as pl
from jax.experimental.pallas import tpu as pltpu
from jax.sharding import PartitionSpec as P

MESH = pl.DeviceIdType.MESH
HD = 128
ZSPLIT = False
EARLY = False
ROWS = 16
CUT = 3
GROUPS, RANKS = 16, 32
SPAN = CUT * HD
PACK = 4
SIDE = PACK * RANKS
NT = (((1,), (1,)), ((), ()))
TN = (((0,), (0,)), ((), ()))
NN = (((1,), (0,)), ((), ()))


def dot(a, b, dims):
    return lax.dot_general(a, b, dims, preferred_element_type=jnp.float32)


def exchange(
    frames, steps, order, q_ref, k_ref, v_ref, go_ref, gw_ref,
    outs_ref, sums_ref, emb_ref,
    raw, stage, moved, rin, ob, xf, of, gwv, gate, part, seen, own, everyone,
    load_sem, zsend, zrecv, ssem, rsem, osend, orecv, asend, arecv, bsend, brecv,
):
    g = lax.axis_index("grp")
    me = lax.axis_index("seq")
    partner = lax.rem(g + GROUPS // 2, GROUPS)
    clip = me // 16
    block = lax.rem(me // 4, 4)
    heads = lax.rem(me, 4)

    loads = [
        pltpu.make_async_copy(ref, raw.at[t], load_sem.at[t])
        for t, ref in enumerate((q_ref, k_ref, v_ref, go_ref))
    ]
    mine = pl.ds(pl.multiple_of(heads * SPAN, HD), SPAN)
    weight = pltpu.make_async_copy(gw_ref.at[:, mine], gwv, load_sem.at[4])
    for load in loads:
        load.start()
    weight.start()

    barrier = pltpu.get_barrier_semaphore()

    def greet(grp, seq):
        pl.semaphore_signal(barrier, inc=1, device_id=(grp, seq), device_id_type=MESH)

    @pl.loop(1, RANKS)
    def _(o):
        greet(g, lax.rem(me + o, RANKS))

    @pl.loop(1, GROUPS)
    def _(o):
        greet(lax.rem(g + o, GROUPS), me)

    for load in loads:
        load.wait()

    def rows(b):
        return pl.ds(pl.multiple_of(b * ROWS, ROWS), ROWS)

    def slot(h, f, t0, n):
        return rin.at[pl.ds(h * (RANKS * 4) + f * 4 + t0, n)]

    def send(h, j, t0, src):
        pltpu.make_async_remote_copy(
            src_ref=src,
            dst_ref=slot(h, me, t0, src.shape[0]),
            send_sem=ssem,
            recv_sem=rsem.at[h],
            device_id=(g, j),
            device_id_type=MESH,
        ).start()

    def keep(h, t0, src):
        pltpu.make_async_copy(src, slot(h, me, t0, src.shape[0]), rsem.at[h]).start()

    def migrate(h, src, dst):
        pltpu.make_async_remote_copy(
            src_ref=src,
            dst_ref=dst,
            send_sem=zsend,
            recv_sem=zrecv.at[h],
            device_id=(partner, me),
            device_id_type=MESH,
        ).start()

    def arrange(h):
        for r in range(2):
            for t in range(4):
                which = order[r, g] if t < 3 else r
                for w in range(4):
                    lanes = slice(w * SPAN + h * HD, w * SPAN + h * HD + HD)
                    stage[h, r, t, w] = raw[t, which, :, lanes]

    def plane(h):
        if not ZSPLIT:
            migrate(h, stage.at[h, 1, pl.ds(0, 3)], moved.at[h])

        @pl.loop(0, RANKS)
        def _(o):
            j = lax.rem(me + o, RANKS)
            b, w = lax.rem(j // 4, 4), lax.rem(j, 4)
            if ZSPLIT:
                @pl.when(lax.rem(o, 2) == 0)
                def _():
                    pb, pw = o // 8, lax.rem(o // 2, 4)
                    migrate(
                        h,
                        stage.at[h, 1, pl.ds(0, 3), pw, rows(pb)],
                        moved.at[h, :, pw, rows(pb)],
                    )

            @pl.when((j < 16) & (o > 0))
            def _():
                send(h, j, 0, stage.at[h, 0, pl.ds(0, 4), w, rows(b)])

            @pl.when((j >= 16) & (o > 0))
            def _():
                send(h, j, 3, stage.at[h, 1, pl.ds(3, 1), w, rows(b)])

            @pl.when((j < 16) & (o == 0))
            def _():
                keep(h, 0, stage.at[h, 0, pl.ds(0, 4), w, rows(b)])

            @pl.when((j >= 16) & (o == 0))
            def _():
                keep(h, 3, stage.at[h, 1, pl.ds(3, 1), w, rows(b)])

    def forward(h):
        pltpu.make_async_copy(moved.at[h], moved.at[h], zrecv.at[h]).wait()

        @pl.loop(0, 16)
        def _(o):
            i = lax.rem(me + o, 16)
            j = 16 + i
            b, w = i // 4, lax.rem(i, 4)

            @pl.when(j != me)
            def _():
                send(h, j, 0, moved.at[h, :, w, rows(b)])

            @pl.when(j == me)
            def _():
                keep(h, 0, moved.at[h, :, w, rows(b)])

    arrange(0)
    pl.semaphore_wait(barrier, RANKS - 1 + GROUPS - 1)
    plane(0)
    arrange(1)
    plane(1)
    arrange(2)
    if EARLY:
        forward(0)
    plane(2)

    half = HD
    row = lax.broadcasted_iota(jnp.int32, (2 * GROUPS, half), 0)
    stamp = jnp.zeros((2 * GROUPS, half), jnp.float32)
    for c in range(2 * GROUPS):
        src = c // 2 if c % 2 == 0 else (c // 2 + GROUPS // 2) % GROUPS
        anchor = src * 2 + order[c % 2, src]
        stamp = jnp.where(row == c, steps[anchor].astype(jnp.float32), stamp)
    k = lax.broadcasted_iota(jnp.int32, (2 * GROUPS, half), 1).astype(jnp.float32)
    angle = stamp * jnp.exp(-math.log(10000.0) * k / half)
    emb_ref[:, :half] = jnp.cos(angle)
    emb_ref[:, half:] = jnp.sin(angle)
    weight.wait()
    gates = lax.dot_general(
        emb_ref[...],
        gwv[...].astype(jnp.float32),
        NN,
        precision=lax.Precision.HIGHEST,
        preferred_element_type=jnp.float32,
    )
    pick = lax.broadcasted_iota(jnp.int32, gates.shape, 0) == g * 2 + clip
    gate[...] = jnp.broadcast_to(
        jnp.sum(jnp.where(pick, gates, 0.0), axis=0, keepdims=True), gate.shape
    )
    source = jnp.where(clip == 0, g, partner)
    count = frames[source * 2 + order[clip, source]]

    if not EARLY:
        forward(0)
    forward(1)
    forward(2)

    line = lax.broadcasted_iota(jnp.int32, (SIDE, SIDE), 0)
    lane = lax.broadcasted_iota(jnp.int32, (SIDE, SIDE), 1)
    live = (line // RANKS == lane // RANKS) & (lax.rem(lane, RANKS) < count)
    asks = (
        lax.rem(lax.broadcasted_iota(jnp.int32, (SIDE, HD), 0), RANKS) < count
    ).astype(jnp.float32)
    scale = HD ** (-0.5)

    @pl.loop(0, CUT)
    def _(h):
        base = h * (RANKS * 4)
        pltpu.make_async_copy(
            rin.at[pl.ds(base, RANKS * 4)], rin.at[pl.ds(base, RANKS * 4)], rsem.at[h]
        ).wait()
        for f in range(RANKS):
            for t in range(4):
                xf[t, f * ROWS : (f + 1) * ROWS, :] = rin[base + f * 4 + t].astype(jnp.float32)
        lanes = pl.ds(pl.multiple_of(h * HD, HD), HD)
        gate_h = gate[0:1, lanes]
        total = jnp.zeros((1, HD), jnp.float32)
        for s in range(ROWS // PACK):

            def take(t):
                return jnp.concatenate(
                    [xf[t, pl.ds(s * PACK + p, RANKS, stride=ROWS), :] for p in range(PACK)], axis=0
                )

            def put(t, value):
                for p in range(PACK):
                    of[t, pl.ds(s * PACK + p, RANKS, stride=ROWS), :] = value[
                        p * RANKS : (p + 1) * RANKS
                    ]

            query = take(0).astype(jnp.bfloat16)
            key = take(1).astype(jnp.bfloat16)
            value = take(2).astype(jnp.bfloat16)
            cotan = take(3)
            scores = jnp.where(live, dot(query, key, NT) * scale, -jnp.inf)
            top = jnp.max(scores, axis=-1, keepdims=True)
            expo = jnp.where(live, jnp.exp(scores - top), 0.0)
            probs = expo / jnp.sum(expo, axis=-1, keepdims=True)
            probs_b = probs.astype(jnp.bfloat16)
            attn = dot(probs_b, value, NN) * asks
            put(0, gate_h * attn)
            total = total + jnp.sum(cotan * attn, axis=0, keepdims=True)
            grad_a = (cotan * gate_h * asks).astype(jnp.bfloat16)
            put(3, dot(probs_b, grad_a, TN))
            dprobs = dot(grad_a, value, NT)
            diag = jnp.sum(probs * dprobs, axis=-1, keepdims=True)
            dscores = (probs * (dprobs - diag)).astype(jnp.bfloat16)
            put(1, dot(dscores, key, NN) * scale)
            put(2, dot(dscores, query, TN) * scale)
        part[0:1, lanes] = total
        for f in range(RANKS):
            for t in range(4):
                ob[base + f * 4 + t] = of[t, f * ROWS : (f + 1) * ROWS, :].astype(jnp.bfloat16)

        @pl.when(h == CUT - 1)
        def _():
            seen[me] = part[...]

            @pl.loop(1, RANKS)
            def _(o):
                pltpu.make_async_remote_copy(
                    src_ref=part,
                    dst_ref=seen.at[me],
                    send_sem=asend,
                    recv_sem=arecv,
                    device_id=(g, lax.rem(me + o, RANKS)),
                    device_id_type=MESH,
                ).start()

        place = outs_ref.at[
            :,
            clip,
            pl.ds(pl.multiple_of(block * ROWS, ROWS), ROWS),
            pl.ds(pl.multiple_of(heads * SPAN + h * HD, HD), HD),
        ]

        @pl.loop(1, RANKS)
        def _(o):
            f = lax.rem(me + o, RANKS)
            pltpu.make_async_remote_copy(
                src_ref=ob.at[pl.ds(base + f * 4, 4)],
                dst_ref=place,
                send_sem=osend,
                recv_sem=orecv,
                device_id=(g, f),
                device_id_type=MESH,
            ).start()

        pltpu.make_async_copy(ob.at[pl.ds(base + me * 4, 4)], place, orecv).start()

    few = seen.at[pl.ds(0, RANKS - 1)]
    pltpu.make_async_copy(few, few, arecv).wait()
    for r in range(2):
        for w in range(4):
            acc = seen[r * 16 + w]
            for b in range(1, 4):
                acc = acc + seen[r * 16 + b * 4 + w]
            own[w * 2 + r : w * 2 + r + 1, :] = acc
    everyone[g] = own[...]

    @pl.loop(1, GROUPS)
    def _(o):
        pltpu.make_async_remote_copy(
            src_ref=own,
            dst_ref=everyone.at[g],
            send_sem=bsend,
            recv_sem=brecv,
            device_id=(lax.rem(g + o, GROUPS), me),
            device_id_type=MESH,
        ).start()

    others = everyone.at[pl.ds(0, GROUPS - 1)]
    pltpu.make_async_copy(others, others, brecv).wait()
    for i in range(GROUPS):
        for w in range(4):
            sums_ref[w, 2 * i : 2 * i + 2, :] = everyone[i, 2 * w : 2 * w + 2, :]

    def drain(sem, ref):
        pltpu.make_async_copy(ref, ref, sem).wait()

    drain(asend, few)
    drain(bsend, others)

    drain(zsend, moved)
    drain(ssem, rin.at[pl.ds(0, CUT * (RANKS - 1) * 4)])
    drain(osend, rin.at[pl.ds(0, CUT * (RANKS - 1) * 4)])
    drain(orecv, outs_ref)


def finish(outs_ref, sums_ref, emb_ref, o_ref, q_ref, k_ref, v_ref, gg_ref, sem):
    copies = [
        pltpu.make_async_copy(outs_ref.at[t], ref, sem.at[t])
        for t, ref in enumerate((o_ref, q_ref, k_ref, v_ref))
    ]
    for copy in copies:
        copy.start()
    emb = emb_ref[...]
    for w in range(4):
        clips = sums_ref[w]
        gg_ref[:, w * SPAN : (w + 1) * SPAN] = lax.dot_general(
            emb,
            clips,
            TN,
            precision=lax.Precision.HIGHEST,
            preferred_element_type=jnp.float32,
        ).astype(jnp.bfloat16)
    for copy in copies:
        copy.wait()


def body(queries, keys, values, grad_out, frames, timesteps, order, gate_weight):
    clips, fr_dev, spots, width = queries.shape
    flat = (clips, spots, width)
    any_space = pl.BlockSpec(memory_space=pl.ANY)
    smem = pl.BlockSpec(memory_space=pltpu.SMEM)
    vmem = pl.BlockSpec(memory_space=pltpu.VMEM)
    bf16, f32 = jnp.bfloat16, jnp.float32
    dma = pltpu.SemaphoreType.DMA
    outs, sums, emb = pl.pallas_call(
        exchange,
        out_shape=(
            jax.ShapeDtypeStruct((4,) + flat, bf16),
            jax.ShapeDtypeStruct((4, 2 * GROUPS, SPAN), f32),
            jax.ShapeDtypeStruct((2 * GROUPS, 2 * HD), f32),
        ),
        in_specs=[smem] * 3 + [any_space] * 5,
        out_specs=(any_space, vmem, vmem),
        scratch_shapes=[
            pltpu.VMEM((4,) + flat, bf16),
            pltpu.VMEM((CUT, 2, 4, 4, spots, HD), bf16),
            pltpu.VMEM((CUT, 3, 4, spots, HD), bf16),
            pltpu.VMEM((CUT * RANKS * 4, ROWS, HD), bf16),
            pltpu.VMEM((CUT * RANKS * 4, ROWS, HD), bf16),
            pltpu.VMEM((4, RANKS * ROWS, HD), f32),
            pltpu.VMEM((4, RANKS * ROWS, HD), f32),
            pltpu.VMEM((gate_weight.shape[0], SPAN), bf16),
            pltpu.VMEM((8, SPAN), f32),
            pltpu.VMEM((1, SPAN), f32),
            pltpu.VMEM((RANKS, 1, SPAN), f32),
            pltpu.VMEM((8, SPAN), f32),
            pltpu.VMEM((GROUPS, 8, SPAN), f32),
            dma((5,)),
            dma,
            dma((CUT,)),
            dma,
            dma((CUT,)),
            dma,
            dma,
            dma,
            dma,
            dma,
            dma,
        ],
        compiler_params=pltpu.CompilerParams(
            collective_id=0, has_side_effects=True, vmem_limit_bytes=32 << 20
        ),
    )(
        frames,
        timesteps,
        order.T,
        pltpu.with_memory_space_constraint(queries.reshape(flat), pltpu.HBM),
        pltpu.with_memory_space_constraint(keys.reshape(flat), pltpu.HBM),
        pltpu.with_memory_space_constraint(values.reshape(flat), pltpu.HBM),
        pltpu.with_memory_space_constraint(grad_out.reshape(flat), pltpu.HBM),
        pltpu.with_memory_space_constraint(gate_weight, pltpu.HBM),
    )
    results = pl.pallas_call(
        finish,
        out_shape=tuple(jax.ShapeDtypeStruct(flat, bf16) for _ in range(4))
        + (jax.ShapeDtypeStruct(gate_weight.shape, bf16),),
        in_specs=[any_space, vmem, vmem],
        out_specs=(any_space,) * 4 + (vmem,),
        scratch_shapes=[dma((4,))],
        compiler_params=pltpu.CompilerParams(vmem_limit_bytes=32 << 20),
    )(outs, sums, emb)
    back = tuple(x.reshape(clips, fr_dev, spots, width) for x in results[:4])
    return back + (results[4],)


def solution(mesh):
    split = P("grp", "seq", None, None)
    return jax.shard_map(
        body,
        mesh=mesh,
        in_specs=(split,) * 4 + (P(),) * 4,
        out_specs=(split,) * 4 + (P(),),
        check_vma=False,
    )
```

```python
import functools
import math

import jax
import jax.numpy as jnp
from jax import lax
from jax.experimental import pallas as pl
from jax.experimental.pallas import tpu as pltpu
from jax.sharding import PartitionSpec as P

MESH = pl.DeviceIdType.MESH
HD = 128
ROWS = 16
CUT = 3
GROUPS, RANKS = 16, 32
SPAN = CUT * HD
PACK = 4
SIDE = PACK * RANKS
NT = (((1,), (1,)), ((), ()))
TN = (((0,), (0,)), ((), ()))
NN = (((1,), (0,)), ((), ()))


def dot(a, b, dims):
    return lax.dot_general(a, b, dims, preferred_element_type=jnp.float32)


def exchange(
    frames_ref, steps_ref, order_ref, q_ref, k_ref, v_ref, go_ref, gw_ref,
    outs_ref, sums_ref, emb_ref,
    raw, stage, moved, rin, ob, xf, of, gwv, gate, part, seen, own, everyone,
    frames, steps, order, load_sem, zsend, zrecv, ssem, rsem, osend, orecv, asend, arecv, bsend, brecv,
):
    g = lax.axis_index("grp")
    me = lax.axis_index("seq")
    partner = lax.rem(g + GROUPS // 2, GROUPS)

    def unit(h, j):
        ends = (lax.div(h, 2), lax.div(j, 8), lax.rem(j, 8))
        middle = (lax.div(j, 16), lax.rem(lax.div(j, 4), 4), 8 + lax.rem(j, 4))
        return tuple(jnp.where(h == 1, m, e) for m, e in zip(middle, ends))

    loads = [
        pltpu.make_async_copy(ref, raw.at[t], load_sem.at[t])
        for t, ref in enumerate((q_ref, k_ref, v_ref, go_ref))
    ]
    weights = [
        pltpu.make_async_copy(
            gw_ref.at[:, pl.ds(pl.multiple_of(unit(h, me)[2] * HD, HD), HD)],
            gwv.at[h],
            load_sem.at[8 + h],
        )
        for h in range(2)
    ]
    loads += [
        pltpu.make_async_copy(ref, small, load_sem.at[5 + t])
        for t, (ref, small) in enumerate(
            ((frames_ref, frames), (steps_ref, steps), (order_ref, order))
        )
    ]
    for load in loads:
        load.start()
    for weight in weights:
        weight.start()

    barrier = pltpu.get_barrier_semaphore()

    def greet(grp, seq):
        pl.semaphore_signal(barrier, inc=1, device_id=(grp, seq), device_id_type=MESH)

    @pl.loop(1, RANKS)
    def _(o):
        greet(g, lax.rem(me + o, RANKS))

    @pl.loop(1, GROUPS)
    def _(o):
        greet(lax.rem(g + o, GROUPS), me)

    for load in loads:
        load.wait()

    def rows(b):
        return pl.ds(pl.multiple_of(b * ROWS, ROWS), ROWS)

    def slot(h, f, t0, n):
        return rin.at[pl.ds(h * (RANKS * 4) + f * 4 + t0, n)]

    def send(h, j, t0, src):
        pltpu.make_async_remote_copy(
            src_ref=src,
            dst_ref=slot(h, me, t0, src.shape[0]),
            send_sem=ssem,
            recv_sem=rsem.at[h],
            device_id=(g, j),
            device_id_type=MESH,
        ).start()

    def keep(h, j, t0, src):
        pltpu.make_async_copy(src, slot(h, me, t0, src.shape[0]), rsem.at[h]).start()

    def migrate(h, src, dst):
        pltpu.make_async_remote_copy(
            src_ref=src,
            dst_ref=dst,
            send_sem=zsend,
            recv_sem=zrecv.at[h],
            device_id=(partner, me),
            device_id_type=MESH,
        ).start()

    def arrange(r, tensors, heads):
        for t in tensors:
            which = order[r, g] if t < 3 else r
            for w in heads:
                stage[r, t, w] = raw[t, which, :, w * HD : (w + 1) * HD]

    def plane(h):
        def whole(j, to):
            _, b, w = unit(h, j)
            to(h, j, 0, stage.at[0, :, w, rows(b)])

        def cotangent(j, to):
            _, b, w = unit(h, j)
            to(h, j, 3, stage.at[1, pl.ds(3, 1), w, rows(b)])

        def either(j, to):
            if h == 0:
                whole(j, to)
            elif h == 2:
                cotangent(j, to)
            else:
                pl.when(j < 16)(lambda: whole(j, to))
                pl.when(j >= 16)(lambda: cotangent(j, to))

        @pl.loop(1, RANKS)
        def _(o):
            either(lax.rem(me + o, RANKS), send)

        either(me, keep)

    def forward(h):
        few = slice(8, 12) if h == 1 else slice(0, 8)
        came = moved.at[:, few]
        pltpu.make_async_copy(came, came, zrecv.at[h - 1]).wait()

        def onward(j, to):
            _, b, w = unit(h, j)
            to(h, j, 0, moved.at[:, w, rows(b)])

        @pl.loop(0, 16 if h == 1 else RANKS)
        def _(o):
            j = 16 + lax.rem(me + o, 16) if h == 1 else lax.rem(me + o, RANKS)
            pl.when(j != me)(lambda: onward(j, send))
            pl.when(j == me)(lambda: onward(j, keep))

    arrange(1, range(3), range(12))
    pl.semaphore_wait(barrier, RANKS - 1 + GROUPS - 1)
    migrate(0, stage.at[1, pl.ds(0, 3), 8:12], moved.at[:, 8:12])
    migrate(1, stage.at[1, pl.ds(0, 3), 0:8], moved.at[:, 0:8])
    arrange(0, range(4), range(8))
    plane(0)
    arrange(0, range(4), range(8, 12))
    arrange(1, range(3, 4), range(12))
    plane(1)
    plane(2)

    half = HD
    row = lax.broadcasted_iota(jnp.int32, (2 * GROUPS, half), 0)
    stamp = jnp.zeros((2 * GROUPS, half), jnp.float32)
    for c in range(2 * GROUPS):
        src = c // 2 if c % 2 == 0 else (c // 2 + GROUPS // 2) % GROUPS
        anchor = src * 2 + order[c % 2, src]
        stamp = jnp.where(row == c, steps[anchor].astype(jnp.float32), stamp)
    k = lax.broadcasted_iota(jnp.int32, (2 * GROUPS, half), 1).astype(jnp.float32)
    angle = stamp * jnp.exp(-math.log(10000.0) * k / half)
    emb_ref[:, :half] = jnp.cos(angle)
    emb_ref[:, half:] = jnp.sin(angle)
    for weight in weights:
        weight.wait()
    row = lax.broadcasted_iota(jnp.int32, (2 * GROUPS, HD), 0)
    for h in range(CUT):
        gates = lax.dot_general(
            emb_ref[...],
            gwv[h % 2].astype(jnp.float32),
            NN,
            precision=lax.Precision.HIGHEST,
            preferred_element_type=jnp.float32,
        )
        pick = row == g * 2 + unit(h, me)[0]
        gate[h] = jnp.sum(jnp.where(pick, gates, 0.0), axis=0, keepdims=True)

    forward(1)
    forward(2)

    line = lax.broadcasted_iota(jnp.int32, (SIDE, SIDE), 0)
    lane = lax.broadcasted_iota(jnp.int32, (SIDE, SIDE), 1)
    scale = HD ** (-0.5)

    @pl.loop(0, CUT)
    def _(h):
        base = h * (RANKS * 4)
        pltpu.make_async_copy(
            rin.at[pl.ds(base, RANKS * 4)], rin.at[pl.ds(base, RANKS * 4)], rsem.at[h]
        ).wait()
        for f in range(RANKS):
            for t in range(4):
                xf[t, f * ROWS : (f + 1) * ROWS, :] = rin[base + f * 4 + t].astype(jnp.float32)
        lanes = pl.ds(pl.multiple_of(h * HD, HD), HD)
        gate_h = gate[h]
        clip, block, head = unit(h, me)
        source = jnp.where(clip == 0, g, partner)
        count = frames[source * 2 + order[clip, source]]
        live = (line // RANKS == lane // RANKS) & (lax.rem(lane, RANKS) < count)
        asks = (lax.rem(line, RANKS) < count).astype(jnp.float32)
        total = jnp.zeros((1, HD), jnp.float32)
        for s in range(ROWS // PACK):

            def take(t):
                return jnp.concatenate(
                    [xf[t, pl.ds(s * PACK + p, RANKS, stride=ROWS), :] for p in range(PACK)], axis=0
                )

            def put(t, value):
                for p in range(PACK):
                    of[t, pl.ds(s * PACK + p, RANKS, stride=ROWS), :] = value[
                        p * RANKS : (p + 1) * RANKS
                    ]

            query = take(0).astype(jnp.bfloat16)
            key = take(1).astype(jnp.bfloat16)
            value = take(2).astype(jnp.bfloat16)
            cotan = take(3)
            scores = jnp.where(live, dot(query, key, NT) * scale, -jnp.inf)
            top = jnp.max(scores, axis=-1, keepdims=True)
            expo = jnp.where(live, jnp.exp(scores - top), 0.0)
            probs = expo / jnp.sum(expo, axis=-1, keepdims=True)
            probs_b = probs.astype(jnp.bfloat16)
            attn = dot(probs_b, value, NN) * asks
            put(0, gate_h * attn)
            total = total + jnp.sum(cotan * attn, axis=0, keepdims=True)
            grad_a = (cotan * gate_h * asks).astype(jnp.bfloat16)
            put(3, dot(probs_b, grad_a, TN))
            dprobs = dot(grad_a, value, NT)
            diag = jnp.sum(probs * dprobs, axis=-1, keepdims=True)
            dscores = (probs * (dprobs - diag)).astype(jnp.bfloat16)
            put(1, dot(dscores, key, NN) * scale)
            put(2, dot(dscores, query, TN) * scale)
        part[0:1, lanes] = total
        for f in range(RANKS):
            for t in range(4):
                ob[base + f * 4 + t] = of[t, f * ROWS : (f + 1) * ROWS, :].astype(jnp.bfloat16)

        @pl.when(h == CUT - 1)
        def _():
            seen[me] = part[...]

            @pl.loop(1, RANKS)
            def _(o):
                pltpu.make_async_remote_copy(
                    src_ref=part,
                    dst_ref=seen.at[me],
                    send_sem=asend,
                    recv_sem=arecv,
                    device_id=(g, lax.rem(me + o, RANKS)),
                    device_id_type=MESH,
                ).start()

        place = outs_ref.at[
            :,
            clip,
            pl.ds(pl.multiple_of(block * ROWS, ROWS), ROWS),
            pl.ds(pl.multiple_of(head * HD, HD), HD),
        ]

        @pl.loop(1, RANKS)
        def _(o):
            f = lax.rem(me + o, RANKS)
            pltpu.make_async_remote_copy(
                src_ref=ob.at[pl.ds(base + f * 4, 4)],
                dst_ref=place,
                send_sem=osend,
                recv_sem=orecv,
                device_id=(g, f),
                device_id_type=MESH,
            ).start()

        pltpu.make_async_copy(ob.at[pl.ds(base + me * 4, 4)], place, orecv).start()

    few = seen.at[pl.ds(0, RANKS - 1)]
    pltpu.make_async_copy(few, few, arecv).wait()
    for r in range(2):
        for w in range(12):
            ranks = [b * 8 + w if w < 8 else r * 16 + b * 4 + w - 8 for b in range(4)]
            h = 1 if w >= 8 else 2 * r
            acc = sum(seen[k, :, h * HD : (h + 1) * HD] for k in ranks)
            own[w // 3 * 2 + r : w // 3 * 2 + r + 1, w % 3 * HD : (w % 3 + 1) * HD] = acc
    everyone[g] = own[...]

    @pl.loop(1, GROUPS)
    def _(o):
        pltpu.make_async_remote_copy(
            src_ref=own,
            dst_ref=everyone.at[g],
            send_sem=bsend,
            recv_sem=brecv,
            device_id=(lax.rem(g + o, GROUPS), me),
            device_id_type=MESH,
        ).start()

    others = everyone.at[pl.ds(0, GROUPS - 1)]
    pltpu.make_async_copy(others, others, brecv).wait()
    for i in range(GROUPS):
        for w in range(4):
            sums_ref[w, 2 * i : 2 * i + 2, :] = everyone[i, 2 * w : 2 * w + 2, :]

    def drain(sem, ref):
        pltpu.make_async_copy(ref, ref, sem).wait()

    drain(asend, few)
    drain(bsend, others)

    drain(zsend, moved)
    drain(ssem, rin.at[pl.ds(0, CUT * (RANKS - 1) * 4)])
    drain(osend, rin.at[pl.ds(0, CUT * (RANKS - 1) * 4)])
    drain(orecv, outs_ref)


def finish(outs_ref, sums_ref, emb_ref, o_ref, q_ref, k_ref, v_ref, gg_ref, sem):
    copies = [
        pltpu.make_async_copy(outs_ref.at[t], ref, sem.at[t])
        for t, ref in enumerate((o_ref, q_ref, k_ref, v_ref))
    ]
    for copy in copies:
        copy.start()
    emb = emb_ref[...]
    for w in range(4):
        clips = sums_ref[w]
        gg_ref[:, w * SPAN : (w + 1) * SPAN] = lax.dot_general(
            emb,
            clips,
            TN,
            precision=lax.Precision.HIGHEST,
            preferred_element_type=jnp.float32,
        ).astype(jnp.bfloat16)
    for copy in copies:
        copy.wait()


def body(queries, keys, values, grad_out, frames, timesteps, order, gate_weight):
    clips, fr_dev, spots, width = queries.shape
    flat = (clips, spots, width)
    any_space = pl.BlockSpec(memory_space=pl.ANY)
    vmem = pl.BlockSpec(memory_space=pltpu.VMEM)
    bf16, f32 = jnp.bfloat16, jnp.float32
    dma = pltpu.SemaphoreType.DMA
    outs, sums, emb = pl.pallas_call(
        exchange,
        out_shape=(
            jax.ShapeDtypeStruct((4,) + flat, bf16),
            jax.ShapeDtypeStruct((4, 2 * GROUPS, SPAN), f32),
            jax.ShapeDtypeStruct((2 * GROUPS, 2 * HD), f32),
        ),
        in_specs=[any_space] * 8,
        out_specs=(any_space, vmem, vmem),
        scratch_shapes=[
            pltpu.VMEM((4,) + flat, bf16),
            pltpu.VMEM((2, 4, 12, spots, HD), bf16),
            pltpu.VMEM((3, 12, spots, HD), bf16),
            pltpu.VMEM((CUT * RANKS * 4, ROWS, HD), bf16),
            pltpu.VMEM((CUT * RANKS * 4, ROWS, HD), bf16),
            pltpu.VMEM((4, RANKS * ROWS, HD), f32),
            pltpu.VMEM((4, RANKS * ROWS, HD), f32),
            pltpu.VMEM((2, gate_weight.shape[0], HD), bf16),
            pltpu.VMEM((CUT, 1, HD), f32),
            pltpu.VMEM((1, SPAN), f32),
            pltpu.VMEM((RANKS, 1, SPAN), f32),
            pltpu.VMEM((8, SPAN), f32),
            pltpu.VMEM((GROUPS, 8, SPAN), f32),
            pltpu.SMEM((2 * GROUPS,), jnp.int32),
            pltpu.SMEM((2 * GROUPS,), jnp.int32),
            pltpu.SMEM((2, GROUPS), jnp.int32),
            dma((10,)),
            dma,
            dma((2,)),
            dma,
            dma((CUT,)),
            dma,
            dma,
            dma,
            dma,
            dma,
            dma,
        ],
        compiler_params=pltpu.CompilerParams(
            collective_id=0, has_side_effects=True, vmem_limit_bytes=32 << 20
        ),
    )(
        pltpu.with_memory_space_constraint(frames, pltpu.HBM),
        pltpu.with_memory_space_constraint(timesteps, pltpu.HBM),
        pltpu.with_memory_space_constraint(order.T, pltpu.HBM),
        pltpu.with_memory_space_constraint(queries.reshape(flat), pltpu.HBM),
        pltpu.with_memory_space_constraint(keys.reshape(flat), pltpu.HBM),
        pltpu.with_memory_space_constraint(values.reshape(flat), pltpu.HBM),
        pltpu.with_memory_space_constraint(grad_out.reshape(flat), pltpu.HBM),
        pltpu.with_memory_space_constraint(gate_weight, pltpu.HBM),
    )
    results = pl.pallas_call(
        finish,
        out_shape=tuple(jax.ShapeDtypeStruct(flat, bf16) for _ in range(4))
        + (jax.ShapeDtypeStruct(gate_weight.shape, bf16),),
        in_specs=[any_space, vmem, vmem],
        out_specs=(any_space,) * 4 + (vmem,),
        scratch_shapes=[dma((4,))],
        compiler_params=pltpu.CompilerParams(vmem_limit_bytes=32 << 20),
    )(outs, sums, emb)
    back = tuple(x.reshape(clips, fr_dev, spots, width) for x in results[:4])
    return back + (results[4],)


def solution(mesh):
    split = P("grp", "seq", None, None)
    return jax.shard_map(
        body,
        mesh=mesh,
        in_specs=(split,) * 4 + (P(),) * 4,
        out_specs=(split,) * 4 + (P(),),
        check_vma=False,
    )
```

```python
import functools
import math

import jax
import jax.numpy as jnp
from jax import lax
from jax.experimental import pallas as pl
from jax.experimental.pallas import tpu as pltpu
from jax.sharding import PartitionSpec as P

MESH = pl.DeviceIdType.MESH
HD = 128
ROWS = 16
CUT = 3
GROUPS, RANKS = 16, 32
SPAN = CUT * HD
PACK = 4
SIDE = PACK * RANKS
NT = (((1,), (1,)), ((), ()))
TN = (((0,), (0,)), ((), ()))
NN = (((1,), (0,)), ((), ()))


def dot(a, b, dims):
    return lax.dot_general(a, b, dims, preferred_element_type=jnp.float32)


def exchange(
    frames_ref, steps_ref, order_ref, q_ref, k_ref, v_ref, go_ref, gw_ref,
    outs_ref, gg_ref,
    emb_ref, raw, stage, moved, rin, ob, xf, of, gwv, gate, part, seen, own, everyone,
    frames, steps, order, load_sem, zsend, zrecv, ssem, rsem, osend, orecv, asend, arecv, bsend, brecv,
):
    g = lax.axis_index("grp")
    me = lax.axis_index("seq")
    partner = lax.rem(g + GROUPS // 2, GROUPS)

    def unit(h, j):
        ends = (lax.div(h, 2), lax.div(j, 8), lax.rem(j, 8))
        middle = (lax.div(j, 16), lax.rem(lax.div(j, 4), 4), 8 + lax.rem(j, 4))
        return tuple(jnp.where(h == 1, m, e) for m, e in zip(middle, ends))

    loads = [
        pltpu.make_async_copy(ref, raw.at[t], load_sem.at[t])
        for t, ref in enumerate((q_ref, k_ref, v_ref, go_ref))
    ]
    weights = [
        pltpu.make_async_copy(
            gw_ref.at[:, pl.ds(pl.multiple_of(unit(h, me)[2] * HD, HD), HD)],
            gwv.at[h],
            load_sem.at[8 + h],
        )
        for h in range(2)
    ]
    loads += [
        pltpu.make_async_copy(ref, small, load_sem.at[5 + t])
        for t, (ref, small) in enumerate(
            ((frames_ref, frames), (steps_ref, steps), (order_ref, order))
        )
    ]
    for load in loads:
        load.start()
    for weight in weights:
        weight.start()

    barrier = pltpu.get_barrier_semaphore()

    def greet(grp, seq):
        pl.semaphore_signal(barrier, inc=1, device_id=(grp, seq), device_id_type=MESH)

    @pl.loop(1, RANKS)
    def _(o):
        greet(g, lax.rem(me + o, RANKS))

    @pl.loop(1, GROUPS)
    def _(o):
        greet(lax.rem(g + o, GROUPS), me)

    for load in loads:
        load.wait()

    def rows(b):
        return pl.ds(pl.multiple_of(b * ROWS, ROWS), ROWS)

    def slot(h, f, t0, n):
        return rin.at[pl.ds(h * (RANKS * 4) + f * 4 + t0, n)]

    def send(h, j, t0, src):
        pltpu.make_async_remote_copy(
            src_ref=src,
            dst_ref=slot(h, me, t0, src.shape[0]),
            send_sem=ssem,
            recv_sem=rsem.at[h],
            device_id=(g, j),
            device_id_type=MESH,
        ).start()

    def keep(h, j, t0, src):
        pltpu.make_async_copy(src, slot(h, me, t0, src.shape[0]), rsem.at[h]).start()

    def migrate(h, src, dst):
        pltpu.make_async_remote_copy(
            src_ref=src,
            dst_ref=dst,
            send_sem=zsend,
            recv_sem=zrecv.at[h],
            device_id=(partner, me),
            device_id_type=MESH,
        ).start()

    def arrange(r, tensors, heads):
        for t in tensors:
            which = order[r, g] if t < 3 else r
            for w in heads:
                stage[r, t, w] = raw[t, which, :, w * HD : (w + 1) * HD]

    def plane(h):
        def whole(j, to):
            _, b, w = unit(h, j)
            to(h, j, 0, stage.at[0, :, w, rows(b)])

        def cotangent(j, to):
            _, b, w = unit(h, j)
            to(h, j, 3, stage.at[1, pl.ds(3, 1), w, rows(b)])

        def either(j, to):
            if h == 0:
                whole(j, to)
            elif h == 2:
                cotangent(j, to)
            else:
                pl.when(j < 16)(lambda: whole(j, to))
                pl.when(j >= 16)(lambda: cotangent(j, to))

        @pl.loop(1, RANKS)
        def _(o):
            either(lax.rem(me + o, RANKS), send)

        either(me, keep)

    def forward(h):
        few = slice(8, 12) if h == 1 else slice(0, 8)
        came = moved.at[:, few]
        pltpu.make_async_copy(came, came, zrecv.at[h - 1]).wait()

        def onward(j, to):
            _, b, w = unit(h, j)
            to(h, j, 0, moved.at[:, w, rows(b)])

        @pl.loop(0, 16 if h == 1 else RANKS)
        def _(o):
            j = 16 + lax.rem(me + o, 16) if h == 1 else lax.rem(me + o, RANKS)
            pl.when(j != me)(lambda: onward(j, send))
            pl.when(j == me)(lambda: onward(j, keep))

    arrange(1, range(3), range(12))
    pl.semaphore_wait(barrier, RANKS - 1 + GROUPS - 1)
    migrate(0, stage.at[1, pl.ds(0, 3), 8:12], moved.at[:, 8:12])
    migrate(1, stage.at[1, pl.ds(0, 3), 0:8], moved.at[:, 0:8])
    arrange(0, range(4), range(8))
    plane(0)
    arrange(0, range(4), range(8, 12))
    arrange(1, range(3, 4), range(12))
    plane(1)
    plane(2)

    half = HD
    row = lax.broadcasted_iota(jnp.int32, (2 * GROUPS, half), 0)
    stamp = jnp.zeros((2 * GROUPS, half), jnp.float32)
    for c in range(2 * GROUPS):
        src = c // 2 if c % 2 == 0 else (c // 2 + GROUPS // 2) % GROUPS
        anchor = src * 2 + order[c % 2, src]
        stamp = jnp.where(row == c, steps[anchor].astype(jnp.float32), stamp)
    k = lax.broadcasted_iota(jnp.int32, (2 * GROUPS, half), 1).astype(jnp.float32)
    angle = stamp * jnp.exp(-math.log(10000.0) * k / half)
    emb_ref[:, :half] = jnp.cos(angle)
    emb_ref[:, half:] = jnp.sin(angle)
    for weight in weights:
        weight.wait()
    row = lax.broadcasted_iota(jnp.int32, (2 * GROUPS, HD), 0)
    for h in range(CUT):
        gates = lax.dot_general(
            emb_ref[...],
            gwv[h % 2].astype(jnp.float32),
            NN,
            precision=lax.Precision.HIGHEST,
            preferred_element_type=jnp.float32,
        )
        pick = row == g * 2 + unit(h, me)[0]
        gate[h] = jnp.sum(jnp.where(pick, gates, 0.0), axis=0, keepdims=True)

    forward(1)
    forward(2)

    line = lax.broadcasted_iota(jnp.int32, (SIDE, SIDE), 0)
    lane = lax.broadcasted_iota(jnp.int32, (SIDE, SIDE), 1)
    scale = HD ** (-0.5)

    @pl.loop(0, CUT)
    def _(h):
        base = h * (RANKS * 4)
        pltpu.make_async_copy(
            rin.at[pl.ds(base, RANKS * 4)], rin.at[pl.ds(base, RANKS * 4)], rsem.at[h]
        ).wait()
        for f in range(RANKS):
            for t in range(4):
                xf[t, f * ROWS : (f + 1) * ROWS, :] = rin[base + f * 4 + t].astype(jnp.float32)
        lanes = pl.ds(pl.multiple_of(h * HD, HD), HD)
        gate_h = gate[h]
        clip, block, head = unit(h, me)
        source = jnp.where(clip == 0, g, partner)
        count = frames[source * 2 + order[clip, source]]
        live = (line // RANKS == lane // RANKS) & (lax.rem(lane, RANKS) < count)
        asks = (lax.rem(line, RANKS) < count).astype(jnp.float32)
        total = jnp.zeros((1, HD), jnp.float32)
        for s in range(ROWS // PACK):

            def take(t):
                return jnp.concatenate(
                    [xf[t, pl.ds(s * PACK + p, RANKS, stride=ROWS), :] for p in range(PACK)], axis=0
                )

            def put(t, value):
                for p in range(PACK):
                    of[t, pl.ds(s * PACK + p, RANKS, stride=ROWS), :] = value[
                        p * RANKS : (p + 1) * RANKS
                    ]

            query = take(0).astype(jnp.bfloat16)
            key = take(1).astype(jnp.bfloat16)
            value = take(2).astype(jnp.bfloat16)
            cotan = take(3)
            scores = jnp.where(live, dot(query, key, NT) * scale, -jnp.inf)
            top = jnp.max(scores, axis=-1, keepdims=True)
            expo = jnp.where(live, jnp.exp(scores - top), 0.0)
            probs = expo / jnp.sum(expo, axis=-1, keepdims=True)
            probs_b = probs.astype(jnp.bfloat16)
            attn = dot(probs_b, value, NN) * asks
            put(0, gate_h * attn)
            total = total + jnp.sum(cotan * attn, axis=0, keepdims=True)
            grad_a = (cotan * gate_h * asks).astype(jnp.bfloat16)
            put(3, dot(probs_b, grad_a, TN))
            dprobs = dot(grad_a, value, NT)
            diag = jnp.sum(probs * dprobs, axis=-1, keepdims=True)
            dscores = (probs * (dprobs - diag)).astype(jnp.bfloat16)
            put(1, dot(dscores, key, NN) * scale)
            put(2, dot(dscores, query, TN) * scale)
        part[0:1, lanes] = total
        for f in range(RANKS):
            for t in range(4):
                ob[base + f * 4 + t] = of[t, f * ROWS : (f + 1) * ROWS, :].astype(jnp.bfloat16)

        @pl.when(h == CUT - 1)
        def _():
            seen[me] = part[...]

            @pl.loop(1, RANKS)
            def _(o):
                pltpu.make_async_remote_copy(
                    src_ref=part,
                    dst_ref=seen.at[me],
                    send_sem=asend,
                    recv_sem=arecv,
                    device_id=(g, lax.rem(me + o, RANKS)),
                    device_id_type=MESH,
                ).start()

        place = outs_ref.at[
            :,
            clip,
            pl.ds(pl.multiple_of(block * ROWS, ROWS), ROWS),
            pl.ds(pl.multiple_of(head * HD, HD), HD),
        ]

        @pl.loop(1, RANKS)
        def _(o):
            f = lax.rem(me + o, RANKS)
            pltpu.make_async_remote_copy(
                src_ref=ob.at[pl.ds(base + f * 4, 4)],
                dst_ref=place,
                send_sem=osend,
                recv_sem=orecv,
                device_id=(g, f),
                device_id_type=MESH,
            ).start()

        pltpu.make_async_copy(ob.at[pl.ds(base + me * 4, 4)], place, orecv).start()

    few = seen.at[pl.ds(0, RANKS - 1)]
    pltpu.make_async_copy(few, few, arecv).wait()
    for r in range(2):
        for w in range(12):
            ranks = [b * 8 + w if w < 8 else r * 16 + b * 4 + w - 8 for b in range(4)]
            h = 1 if w >= 8 else 2 * r
            acc = sum(seen[k, :, h * HD : (h + 1) * HD] for k in ranks)
            own[w // 3 * 2 + r : w // 3 * 2 + r + 1, w % 3 * HD : (w % 3 + 1) * HD] = acc
    everyone[g] = own[...]

    @pl.loop(1, GROUPS)
    def _(o):
        pltpu.make_async_remote_copy(
            src_ref=own,
            dst_ref=everyone.at[g],
            send_sem=bsend,
            recv_sem=brecv,
            device_id=(lax.rem(g + o, GROUPS), me),
            device_id_type=MESH,
        ).start()

    others = everyone.at[pl.ds(0, GROUPS - 1)]
    pltpu.make_async_copy(others, others, brecv).wait()
    for w in range(4):
        clips = jnp.concatenate(
            [everyone[i, 2 * w : 2 * w + 2, :] for i in range(GROUPS)], axis=0
        )
        gg_ref[:, w * SPAN : (w + 1) * SPAN] = lax.dot_general(
            emb_ref[...],
            clips,
            TN,
            precision=lax.Precision.HIGHEST,
            preferred_element_type=jnp.float32,
        ).astype(jnp.bfloat16)

    def drain(sem, ref):
        pltpu.make_async_copy(ref, ref, sem).wait()

    drain(asend, few)
    drain(bsend, others)

    drain(zsend, moved)
    drain(ssem, rin.at[pl.ds(0, CUT * (RANKS - 1) * 4)])
    drain(osend, rin.at[pl.ds(0, CUT * (RANKS - 1) * 4)])
    drain(orecv, outs_ref)


def finish(outs_ref, gg_in, o_ref, q_ref, k_ref, v_ref, gg_ref, sem):
    copies = [
        pltpu.make_async_copy(outs_ref.at[t], ref, sem.at[t])
        for t, ref in enumerate((o_ref, q_ref, k_ref, v_ref))
    ]
    copies.append(pltpu.make_async_copy(gg_in, gg_ref, sem.at[4]))
    for copy in copies:
        copy.start()
    for copy in copies:
        copy.wait()


def body(queries, keys, values, grad_out, frames, timesteps, order, gate_weight):
    clips, fr_dev, spots, width = queries.shape
    flat = (clips, spots, width)
    any_space = pl.BlockSpec(memory_space=pl.ANY)
    vmem = pl.BlockSpec(memory_space=pltpu.VMEM)
    bf16, f32 = jnp.bfloat16, jnp.float32
    dma = pltpu.SemaphoreType.DMA
    outs, product = pl.pallas_call(
        exchange,
        out_shape=(
            jax.ShapeDtypeStruct((4,) + flat, bf16),
            jax.ShapeDtypeStruct(gate_weight.shape, bf16),
        ),
        in_specs=[any_space] * 8,
        out_specs=(any_space, vmem),
        scratch_shapes=[
            pltpu.VMEM((2 * GROUPS, 2 * HD), f32),
            pltpu.VMEM((4,) + flat, bf16),
            pltpu.VMEM((2, 4, 12, spots, HD), bf16),
            pltpu.VMEM((3, 12, spots, HD), bf16),
            pltpu.VMEM((CUT * RANKS * 4, ROWS, HD), bf16),
            pltpu.VMEM((CUT * RANKS * 4, ROWS, HD), bf16),
            pltpu.VMEM((4, RANKS * ROWS, HD), f32),
            pltpu.VMEM((4, RANKS * ROWS, HD), f32),
            pltpu.VMEM((2, gate_weight.shape[0], HD), bf16),
            pltpu.VMEM((CUT, 1, HD), f32),
            pltpu.VMEM((1, SPAN), f32),
            pltpu.VMEM((RANKS, 1, SPAN), f32),
            pltpu.VMEM((8, SPAN), f32),
            pltpu.VMEM((GROUPS, 8, SPAN), f32),
            pltpu.SMEM((2 * GROUPS,), jnp.int32),
            pltpu.SMEM((2 * GROUPS,), jnp.int32),
            pltpu.SMEM((2, GROUPS), jnp.int32),
            dma((10,)),
            dma,
            dma((2,)),
            dma,
            dma((CUT,)),
            dma,
            dma,
            dma,
            dma,
            dma,
            dma,
        ],
        compiler_params=pltpu.CompilerParams(
            collective_id=0, has_side_effects=True, vmem_limit_bytes=32 << 20
        ),
    )(
        pltpu.with_memory_space_constraint(frames, pltpu.HBM),
        pltpu.with_memory_space_constraint(timesteps, pltpu.HBM),
        pltpu.with_memory_space_constraint(order.T, pltpu.HBM),
        pltpu.with_memory_space_constraint(queries.reshape(flat), pltpu.HBM),
        pltpu.with_memory_space_constraint(keys.reshape(flat), pltpu.HBM),
        pltpu.with_memory_space_constraint(values.reshape(flat), pltpu.HBM),
        pltpu.with_memory_space_constraint(grad_out.reshape(flat), pltpu.HBM),
        pltpu.with_memory_space_constraint(gate_weight, pltpu.HBM),
    )
    results = pl.pallas_call(
        finish,
        out_shape=tuple(jax.ShapeDtypeStruct(flat, bf16) for _ in range(4))
        + (jax.ShapeDtypeStruct(gate_weight.shape, bf16),),
        in_specs=[any_space] * 2,
        out_specs=(any_space,) * 5,
        scratch_shapes=[dma((5,))],
        compiler_params=pltpu.CompilerParams(vmem_limit_bytes=32 << 20),
    )(outs, product)
    back = tuple(x.reshape(clips, fr_dev, spots, width) for x in results[:4])
    return back + (results[4],)


def solution(mesh):
    split = P("grp", "seq", None, None)
    return jax.shard_map(
        body,
        mesh=mesh,
        in_specs=(split,) * 4 + (P(),) * 4,
        out_specs=(split,) * 4 + (P(),),
        check_vma=False,
    )
```

```python
import functools
import math

import jax
import jax.numpy as jnp
from jax import lax
from jax.experimental import pallas as pl
from jax.experimental.pallas import tpu as pltpu
from jax.sharding import PartitionSpec as P

MESH = pl.DeviceIdType.MESH
HD = 128
ROWS = 16
CUT = 3
GROUPS, RANKS = 16, 32
SPAN = CUT * HD
PACK = 4
SIDE = PACK * RANKS
NT = (((1,), (1,)), ((), ()))
TN = (((0,), (0,)), ((), ()))
NN = (((1,), (0,)), ((), ()))


def dot(a, b, dims):
    return lax.dot_general(a, b, dims, preferred_element_type=jnp.float32)


def exchange(
    frames_ref, steps_ref, order_ref, q_ref, k_ref, v_ref, go_ref, gw_ref,
    outs_ref, gg_ref,
    emb_ref, raw, stage, moved, rin, ob, xf, of, gwv, gate, part, seen, own, everyone,
    frames, steps, order, load_sem, zsend, zrecv, ssem, rsem, osend, orecv, asend, arecv, bsend, brecv,
):
    g = lax.axis_index("grp")
    me = lax.axis_index("seq")
    partner = lax.rem(g + GROUPS // 2, GROUPS)

    def unit(h, j):
        ends = (lax.div(h, 2), lax.div(j, 8), lax.rem(j, 8))
        middle = (lax.div(j, 16), lax.rem(lax.div(j, 4), 4), 8 + lax.rem(j, 4))
        return tuple(jnp.where(h == 1, m, e) for m, e in zip(middle, ends))

    loads = [
        pltpu.make_async_copy(ref, raw.at[t], load_sem.at[t])
        for t, ref in enumerate((q_ref, k_ref, v_ref, go_ref))
    ]
    weights = [
        pltpu.make_async_copy(
            gw_ref.at[:, pl.ds(pl.multiple_of(unit(h, me)[2] * HD, HD), HD)],
            gwv.at[h],
            load_sem.at[8 + h],
        )
        for h in range(2)
    ]
    loads += [
        pltpu.make_async_copy(ref, small, load_sem.at[5 + t])
        for t, (ref, small) in enumerate(
            ((frames_ref, frames), (steps_ref, steps), (order_ref, order))
        )
    ]
    for load in loads:
        load.start()
    for weight in weights:
        weight.start()

    barrier = pltpu.get_barrier_semaphore()

    def greet(grp, seq):
        pl.semaphore_signal(barrier, inc=1, device_id=(grp, seq), device_id_type=MESH)

    @pl.loop(1, RANKS)
    def _(o):
        greet(g, lax.rem(me + o, RANKS))

    @pl.loop(1, GROUPS)
    def _(o):
        greet(lax.rem(g + o, GROUPS), me)

    for load in loads:
        load.wait()

    def peer(o):
        y, x = lax.div(me, 4) + 3 * lax.rem(o, 8), lax.rem(me, 4) + lax.div(o, 8) + lax.rem(o, 8)
        return lax.rem(y, 8) * 4 + lax.rem(x, 4)

    def rows(b):
        return pl.ds(pl.multiple_of(b * ROWS, ROWS), ROWS)

    def slot(h, f, t0, n):
        return rin.at[pl.ds(h * (RANKS * 4) + f * 4 + t0, n)]

    def send(h, j, t0, src):
        pltpu.make_async_remote_copy(
            src_ref=src,
            dst_ref=slot(h, me, t0, src.shape[0]),
            send_sem=ssem,
            recv_sem=rsem.at[h],
            device_id=(g, j),
            device_id_type=MESH,
        ).start()

    def keep(h, j, t0, src):
        pltpu.make_async_copy(src, slot(h, me, t0, src.shape[0]), rsem.at[h]).start()

    def migrate(h, src, dst):
        pltpu.make_async_remote_copy(
            src_ref=src,
            dst_ref=dst,
            send_sem=zsend,
            recv_sem=zrecv.at[h],
            device_id=(partner, me),
            device_id_type=MESH,
        ).start()

    def arrange(r, tensors, heads):
        for t in tensors:
            which = order[r, g] if t < 3 else r
            for w in heads:
                stage[r, t, w] = raw[t, which, :, w * HD : (w + 1) * HD]

    def plane(h):
        def whole(j, to):
            _, b, w = unit(h, j)
            to(h, j, 0, stage.at[0, :, w, rows(b)])

        def cotangent(j, to):
            _, b, w = unit(h, j)
            to(h, j, 3, stage.at[1, pl.ds(3, 1), w, rows(b)])

        def either(j, to):
            if h == 0:
                whole(j, to)
            elif h == 2:
                cotangent(j, to)
            else:
                pl.when(j < 16)(lambda: whole(j, to))
                pl.when(j >= 16)(lambda: cotangent(j, to))

        @pl.loop(1, RANKS)
        def _(o):
            either(peer(o), send)

        either(me, keep)

    def forward(h):
        few = slice(8, 12) if h == 1 else slice(0, 8)
        came = moved.at[:, few]
        pltpu.make_async_copy(came, came, zrecv.at[h - 1]).wait()

        def onward(j, to):
            _, b, w = unit(h, j)
            to(h, j, 0, moved.at[:, w, rows(b)])

        @pl.loop(0, 16 if h == 1 else RANKS)
        def _(o):
            j = 16 + lax.rem(me + o, 16) if h == 1 else peer(o)
            pl.when(j != me)(lambda: onward(j, send))
            pl.when(j == me)(lambda: onward(j, keep))

    arrange(1, range(3), range(12))
    pl.semaphore_wait(barrier, RANKS - 1 + GROUPS - 1)
    migrate(0, stage.at[1, pl.ds(0, 3), 8:12], moved.at[:, 8:12])
    migrate(1, stage.at[1, pl.ds(0, 3), 0:8], moved.at[:, 0:8])
    arrange(0, range(4), range(8))
    plane(0)
    arrange(0, range(4), range(8, 12))
    arrange(1, range(3, 4), range(12))
    plane(1)
    plane(2)

    half = HD
    row = lax.broadcasted_iota(jnp.int32, (2 * GROUPS, half), 0)
    stamp = jnp.zeros((2 * GROUPS, half), jnp.float32)
    for c in range(2 * GROUPS):
        src = c // 2 if c % 2 == 0 else (c // 2 + GROUPS // 2) % GROUPS
        anchor = src * 2 + order[c % 2, src]
        stamp = jnp.where(row == c, steps[anchor].astype(jnp.float32), stamp)
    k = lax.broadcasted_iota(jnp.int32, (2 * GROUPS, half), 1).astype(jnp.float32)
    angle = stamp * jnp.exp(-math.log(10000.0) * k / half)
    emb_ref[:, :half] = jnp.cos(angle)
    emb_ref[:, half:] = jnp.sin(angle)
    for weight in weights:
        weight.wait()
    row = lax.broadcasted_iota(jnp.int32, (2 * GROUPS, HD), 0)
    for h in range(CUT):
        gates = lax.dot_general(
            emb_ref[...],
            gwv[h % 2].astype(jnp.float32),
            NN,
            precision=lax.Precision.HIGHEST,
            preferred_element_type=jnp.float32,
        )
        pick = row == g * 2 + unit(h, me)[0]
        gate[h] = jnp.sum(jnp.where(pick, gates, 0.0), axis=0, keepdims=True)

    forward(1)
    forward(2)

    line = lax.broadcasted_iota(jnp.int32, (SIDE, SIDE), 0)
    lane = lax.broadcasted_iota(jnp.int32, (SIDE, SIDE), 1)
    scale = HD ** (-0.5)

    @pl.loop(0, CUT)
    def _(h):
        base = h * (RANKS * 4)
        pltpu.make_async_copy(
            rin.at[pl.ds(base, RANKS * 4)], rin.at[pl.ds(base, RANKS * 4)], rsem.at[h]
        ).wait()
        for f in range(RANKS):
            for t in range(4):
                xf[t, f * ROWS : (f + 1) * ROWS, :] = rin[base + f * 4 + t].astype(jnp.float32)
        lanes = pl.ds(pl.multiple_of(h * HD, HD), HD)
        gate_h = gate[h]
        clip, block, head = unit(h, me)
        source = jnp.where(clip == 0, g, partner)
        count = frames[source * 2 + order[clip, source]]
        live = (line // RANKS == lane // RANKS) & (lax.rem(lane, RANKS) < count)
        asks = (lax.rem(line, RANKS) < count).astype(jnp.float32)
        total = jnp.zeros((1, HD), jnp.float32)
        for s in range(ROWS // PACK):

            def take(t):
                return jnp.concatenate(
                    [xf[t, pl.ds(s * PACK + p, RANKS, stride=ROWS), :] for p in range(PACK)], axis=0
                )

            def put(t, value):
                for p in range(PACK):
                    of[t, pl.ds(s * PACK + p, RANKS, stride=ROWS), :] = value[
                        p * RANKS : (p + 1) * RANKS
                    ]

            query = take(0).astype(jnp.bfloat16)
            key = take(1).astype(jnp.bfloat16)
            value = take(2).astype(jnp.bfloat16)
            cotan = take(3)
            scores = jnp.where(live, dot(query, key, NT) * scale, -jnp.inf)
            top = jnp.max(scores, axis=-1, keepdims=True)
            expo = jnp.where(live, jnp.exp(scores - top), 0.0)
            probs = expo / jnp.sum(expo, axis=-1, keepdims=True)
            probs_b = probs.astype(jnp.bfloat16)
            attn = dot(probs_b, value, NN) * asks
            put(0, gate_h * attn)
            total = total + jnp.sum(cotan * attn, axis=0, keepdims=True)
            grad_a = (cotan * gate_h * asks).astype(jnp.bfloat16)
            put(3, dot(probs_b, grad_a, TN))
            dprobs = dot(grad_a, value, NT)
            diag = jnp.sum(probs * dprobs, axis=-1, keepdims=True)
            dscores = (probs * (dprobs - diag)).astype(jnp.bfloat16)
            put(1, dot(dscores, key, NN) * scale)
            put(2, dot(dscores, query, TN) * scale)
        part[0:1, lanes] = total
        for f in range(RANKS):
            for t in range(4):
                ob[base + f * 4 + t] = of[t, f * ROWS : (f + 1) * ROWS, :].astype(jnp.bfloat16)

        @pl.when(h == CUT - 1)
        def _():
            seen[me] = part[...]

            @pl.loop(1, RANKS)
            def _(o):
                pltpu.make_async_remote_copy(
                    src_ref=part,
                    dst_ref=seen.at[me],
                    send_sem=asend,
                    recv_sem=arecv,
                    device_id=(g, lax.rem(me + o, RANKS)),
                    device_id_type=MESH,
                ).start()

        place = outs_ref.at[
            :,
            clip,
            pl.ds(pl.multiple_of(block * ROWS, ROWS), ROWS),
            pl.ds(pl.multiple_of(head * HD, HD), HD),
        ]

        @pl.loop(1, RANKS)
        def _(o):
            f = peer(o)
            pltpu.make_async_remote_copy(
                src_ref=ob.at[pl.ds(base + f * 4, 4)],
                dst_ref=place,
                send_sem=osend,
                recv_sem=orecv,
                device_id=(g, f),
                device_id_type=MESH,
            ).start()

        pltpu.make_async_copy(ob.at[pl.ds(base + me * 4, 4)], place, orecv).start()

    few = seen.at[pl.ds(0, RANKS - 1)]
    pltpu.make_async_copy(few, few, arecv).wait()
    for r in range(2):
        for w in range(12):
            ranks = [b * 8 + w if w < 8 else r * 16 + b * 4 + w - 8 for b in range(4)]
            h = 1 if w >= 8 else 2 * r
            acc = sum(seen[k, :, h * HD : (h + 1) * HD] for k in ranks)
            own[w // 3 * 2 + r : w // 3 * 2 + r + 1, w % 3 * HD : (w % 3 + 1) * HD] = acc
    everyone[g] = own[...]

    @pl.loop(1, GROUPS)
    def _(o):
        pltpu.make_async_remote_copy(
            src_ref=own,
            dst_ref=everyone.at[g],
            send_sem=bsend,
            recv_sem=brecv,
            device_id=(lax.rem(g + o, GROUPS), me),
            device_id_type=MESH,
        ).start()

    others = everyone.at[pl.ds(0, GROUPS - 1)]
    pltpu.make_async_copy(others, others, brecv).wait()
    for w in range(4):
        clips = jnp.concatenate(
            [everyone[i, 2 * w : 2 * w + 2, :] for i in range(GROUPS)], axis=0
        )
        gg_ref[:, w * SPAN : (w + 1) * SPAN] = lax.dot_general(
            emb_ref[...],
            clips,
            TN,
            precision=lax.Precision.HIGHEST,
            preferred_element_type=jnp.float32,
        ).astype(jnp.bfloat16)

    def drain(sem, ref):
        pltpu.make_async_copy(ref, ref, sem).wait()

    drain(asend, few)
    drain(bsend, others)

    drain(zsend, moved)
    drain(ssem, rin.at[pl.ds(0, CUT * (RANKS - 1) * 4)])
    drain(osend, rin.at[pl.ds(0, CUT * (RANKS - 1) * 4)])
    drain(orecv, outs_ref)


def finish(outs_ref, gg_in, o_ref, q_ref, k_ref, v_ref, gg_ref, sem):
    copies = [
        pltpu.make_async_copy(outs_ref.at[t], ref, sem.at[t])
        for t, ref in enumerate((o_ref, q_ref, k_ref, v_ref))
    ]
    copies.append(pltpu.make_async_copy(gg_in, gg_ref, sem.at[4]))
    for copy in copies:
        copy.start()
    for copy in copies:
        copy.wait()


def body(queries, keys, values, grad_out, frames, timesteps, order, gate_weight):
    clips, fr_dev, spots, width = queries.shape
    flat = (clips, spots, width)
    any_space = pl.BlockSpec(memory_space=pl.ANY)
    vmem = pl.BlockSpec(memory_space=pltpu.VMEM)
    bf16, f32 = jnp.bfloat16, jnp.float32
    dma = pltpu.SemaphoreType.DMA
    outs, product = pl.pallas_call(
        exchange,
        out_shape=(
            jax.ShapeDtypeStruct((4,) + flat, bf16),
            jax.ShapeDtypeStruct(gate_weight.shape, bf16),
        ),
        in_specs=[any_space] * 8,
        out_specs=(any_space, vmem),
        scratch_shapes=[
            pltpu.VMEM((2 * GROUPS, 2 * HD), f32),
            pltpu.VMEM((4,) + flat, bf16),
            pltpu.VMEM((2, 4, 12, spots, HD), bf16),
            pltpu.VMEM((3, 12, spots, HD), bf16),
            pltpu.VMEM((CUT * RANKS * 4, ROWS, HD), bf16),
            pltpu.VMEM((CUT * RANKS * 4, ROWS, HD), bf16),
            pltpu.VMEM((4, RANKS * ROWS, HD), f32),
            pltpu.VMEM((4, RANKS * ROWS, HD), f32),
            pltpu.VMEM((2, gate_weight.shape[0], HD), bf16),
            pltpu.VMEM((CUT, 1, HD), f32),
            pltpu.VMEM((1, SPAN), f32),
            pltpu.VMEM((RANKS, 1, SPAN), f32),
            pltpu.VMEM((8, SPAN), f32),
            pltpu.VMEM((GROUPS, 8, SPAN), f32),
            pltpu.SMEM((2 * GROUPS,), jnp.int32),
            pltpu.SMEM((2 * GROUPS,), jnp.int32),
            pltpu.SMEM((2, GROUPS), jnp.int32),
            dma((10,)),
            dma,
            dma((2,)),
            dma,
            dma((CUT,)),
            dma,
            dma,
            dma,
            dma,
            dma,
            dma,
        ],
        compiler_params=pltpu.CompilerParams(
            collective_id=0, has_side_effects=True, vmem_limit_bytes=32 << 20
        ),
    )(
        pltpu.with_memory_space_constraint(frames, pltpu.HBM),
        pltpu.with_memory_space_constraint(timesteps, pltpu.HBM),
        pltpu.with_memory_space_constraint(order.T, pltpu.HBM),
        pltpu.with_memory_space_constraint(queries.reshape(flat), pltpu.HBM),
        pltpu.with_memory_space_constraint(keys.reshape(flat), pltpu.HBM),
        pltpu.with_memory_space_constraint(values.reshape(flat), pltpu.HBM),
        pltpu.with_memory_space_constraint(grad_out.reshape(flat), pltpu.HBM),
        pltpu.with_memory_space_constraint(gate_weight, pltpu.HBM),
    )
    results = pl.pallas_call(
        finish,
        out_shape=tuple(jax.ShapeDtypeStruct(flat, bf16) for _ in range(4))
        + (jax.ShapeDtypeStruct(gate_weight.shape, bf16),),
        in_specs=[any_space] * 2,
        out_specs=(any_space,) * 5,
        scratch_shapes=[dma((5,))],
        compiler_params=pltpu.CompilerParams(vmem_limit_bytes=32 << 20),
    )(outs, product)
    back = tuple(x.reshape(clips, fr_dev, spots, width) for x in results[:4])
    return back + (results[4],)


def solution(mesh):
    split = P("grp", "seq", None, None)
    return jax.shard_map(
        body,
        mesh=mesh,
        in_specs=(split,) * 4 + (P(),) * 4,
        out_specs=(split,) * 4 + (P(),),
        check_vma=False,
    )
```
